128 devices in a mesh: frame: 8 (over z, core), band: 16 (over x, y).
Axes of the slice: x: 4, y: 4, z: 4, core: 2. Of those that a mesh axis runs over, the one named last changes fastest.
Arguments:
- queries: bfloat16 [16, 2048, 3072], P('frame', 'band'), may hold values from -6 to 6
- keys: bfloat16 [16, 2048, 3072], P('frame', 'band'), may hold values from -6 to 6
- values: bfloat16 [16, 2048, 3072], P('frame', 'band'), may hold values from -6 to 6
- head_kind: int32 [24], replicated, may hold values from 0 to 1, as said below
- spatial_mask: int32 [16, 16, 16], P('frame', 'band'), may hold values from 0 to 1, as said below
- temporal_mask: int32 [16, 16, 16], P('band', 'frame'), may hold values from 0 to 1, as said below
Outputs:
- attended: bfloat16 [16, 2048, 3072], P('frame', 'band')
The draws below stay inside these ranges and needn't reach their ends.
Inputs may be any that keep to these rules, and one draw needn't show every extreme that they name: `head_kind`: exactly 16 entries are 1. `spatial_mask`: every diagonal tile (query band equal to key band) is allowed. `temporal_mask`: every diagonal tile (query frame equal to key frame) is allowed.
All inputs are finite; a program needn't handle non-finite values.
Results may differ from the reference program's by a relative error of at most 0.007.
Values may be sent and summed in bfloat16 or wider, within the bound.
A program may use at most 128 MiB of HBM per device.

```python
import math
import jax
import jax.numpy as jnp
from jax import lax

HD = 128
HEADS = 24
SPATIAL = 16
TILE = 128
FRAMES = 16
BANDS = 16


def draw_queries(key, part):
    key = jax.random.fold_in(key, 1)
    shape = (FRAMES, BANDS * TILE, HEADS * HD)
    field = jnp.clip(jax.random.normal(key, shape, jnp.float32), -6.0, 6.0)
    return field.astype(jnp.bfloat16)


def draw_keys(key, part):
    key = jax.random.fold_in(key, 11)
    shape = (FRAMES, BANDS * TILE, HEADS * HD)
    field = jnp.clip(jax.random.normal(key, shape, jnp.float32), -6.0, 6.0)
    return field.astype(jnp.bfloat16)


def draw_head_kind(key, part):
    key = jax.random.fold_in(key, 21)
    shuffled = jax.random.permutation(key, HEADS)
    return (shuffled < SPATIAL).astype(jnp.int32)


def tile_mask(key, outer, count):
    picks = jax.random.randint(jax.random.fold_in(key, 1), (outer, count, count), 0, count)
    limits = jax.random.randint(jax.random.fold_in(key, 2), (outer, count, 1), 1, count + 1)
    diagonal = jnp.eye(count, dtype=jnp.int32)[None] > 0
    return jnp.logical_or(picks < limits, diagonal).astype(jnp.int32)


def draw_spatial_mask(key, part):
    key = jax.random.fold_in(key, 31)
    return tile_mask(key, FRAMES, BANDS)


def draw_temporal_mask(key, part):
    key = jax.random.fold_in(key, 41)
    return tile_mask(key, BANDS, FRAMES)


def block_levels(rng, extent, split, low, top_value):
    level, own = 1.0, jax.random.fold_in(rng, 6)
    for position, parts in split:
        steps = jnp.exp(jax.random.uniform(jax.random.fold_in(own, position), (parts,), jnp.float32, low / len(split), top_value / len(split)))
        level = level * jnp.repeat(steps, extent[position] // parts).reshape([-1 if axis == position else 1 for axis in range(len(extent))])
    return level


def normal_values(rng, extent, spread, limit, cuts=(), held_as=jnp.bfloat16):
    factor_of = block_levels(rng, extent, cuts, -0.22, 0.18) if cuts else 1.0
    entries = jax.random.normal(rng, extent, jnp.float32) * spread * factor_of
    return jnp.minimum(jnp.maximum(entries, -limit), limit).astype(held_as)


def setup_inputs(seed: int = 0) -> dict:
    splits = jax.random.split(jax.random.key(seed), 7)
    return {
        "queries": draw_queries(jax.random.fold_in(splits[6], 71), 0),
        "keys": draw_keys(jax.random.fold_in(splits[6], 71), 0),
        "values": normal_values(splits[2], (FRAMES, BANDS * TILE, HEADS * HD), 1.0, 6.0, ((0, 8), (1, 16))),
        "head_kind": draw_head_kind(jax.random.fold_in(splits[6], 71), 0),
        "spatial_mask": draw_spatial_mask(jax.random.fold_in(splits[6], 71), 0),
        "temporal_mask": draw_temporal_mask(jax.random.fold_in(splits[6], 71), 0),
    }


NEGATIVE = -1e+30

def attend(query, key, value, allowed):
    scores = jnp.einsum('qhd,khd->hqk', query.astype(jnp.float32), key.astype(jnp.float32)) / math.sqrt(HD)
    full = jnp.repeat(jnp.repeat(allowed > 0, TILE, axis=0), TILE, axis=1)
    scores = jnp.where(full[None], scores, NEGATIVE)
    top = lax.optimization_barrier(jnp.max(scores, axis=-1, keepdims=True))
    weights = jnp.where(full[None], jnp.exp(scores - top), 0.0)
    total = lax.optimization_barrier(jnp.sum(weights, axis=-1))
    rounded = lax.optimization_barrier(weights.astype(jnp.bfloat16)).astype(jnp.float32)
    summed = jnp.einsum('hqk,khd->qhd', rounded, value.astype(jnp.float32))
    return summed / jnp.transpose(total)[:, :, None]

def reference(queries, keys, values, head_kind, spatial_mask, temporal_mask):
    frames, tokens, width = queries.shape
    order = jnp.argsort(1 - head_kind, stable=True).astype(jnp.int32)
    back = jnp.argsort(order, stable=True).astype(jnp.int32)
    shaped = [x.reshape(frames, tokens, HEADS, HD) for x in (queries, keys, values)]
    spat = [jnp.take(x, order[:SPATIAL], axis=2) for x in shaped]
    temp = [jnp.take(x, order[SPATIAL:], axis=2) for x in shaped]

    def spatial_frame(items):
        return attend(items[0], items[1], items[2], items[3])
    out_spatial = lax.map(spatial_frame, (spat[0], spat[1], spat[2], spatial_mask))

    def by_band(x):
        x = x.reshape(frames, BANDS, TILE, HEADS - SPATIAL, HD)
        return jnp.transpose(x, (1, 0, 2, 3, 4)).reshape(BANDS, frames * TILE, HEADS - SPATIAL, HD)

    def temporal_band(items):
        return attend(items[0], items[1], items[2], items[3])
    out_temporal = lax.map(temporal_band, (by_band(temp[0]), by_band(temp[1]), by_band(temp[2]), temporal_mask))
    out_temporal = out_temporal.reshape(BANDS, frames, TILE, HEADS - SPATIAL, HD)
    out_temporal = jnp.transpose(out_temporal, (1, 0, 2, 3, 4)).reshape(frames, tokens, HEADS - SPATIAL, HD)
    joined = jnp.concatenate([out_spatial, out_temporal], axis=2)
    joined = jnp.take(joined, back, axis=2)
    return joined.reshape(frames, tokens, width).astype(jnp.bfloat16)
```

```python
import functools
import math

import jax
import jax.numpy as jnp
from jax import lax
from jax.experimental import pallas as pl
from jax.experimental.pallas import tpu as pltpu
from jax.sharding import PartitionSpec as P

MESH = pl.DeviceIdType.MESH
HD = 128
HEADS = 24
SPATIAL = 16
TEMPORAL = HEADS - SPATIAL
TILE = 128
TILES = 16
TOKENS = TILES * TILE
NEGATIVE = -1e30
EXPONENT = math.log2(math.e) / math.sqrt(HD)
PAD = 16
QROWS = TILE + PAD
CHUNK = 512
NT = (((1,), (1,)), ((), ()))
BF16 = jnp.bfloat16
F32 = jnp.float32

BAND_STEPS = (
    (0, 0), (1, 0), (0, 3), (3, 0), (0, 1), (2, 0), (0, 2), (1, 1),
    (3, 3), (1, 3), (3, 1), (2, 1), (1, 2), (2, 3), (3, 2), (2, 2),
)
FRAME_STEPS = ((0, 0), (0, 1), (1, 0), (3, 0), (1, 1), (3, 1), (2, 0), (2, 1))


def pick(table, index):
    if isinstance(index, int):
        return table[index]
    value = jnp.int32(table[0])
    for place in range(1, len(table)):
        value = jnp.where(index == place, jnp.int32(table[place]), value)
    return value


def band_at(me, index, sign):
    dx = pick([s[0] for s in BAND_STEPS], index)
    dy = pick([s[1] for s in BAND_STEPS], index)
    return (me // 4 + 4 + sign * dx) % 4 * 4 + (me % 4 + 4 + sign * dy) % 4


def frame_at(me, index, sign):
    dz = pick([s[0] for s in FRAME_STEPS], index)
    dc = pick([s[1] for s in FRAME_STEPS], index)
    return (me // 2 + 4 + sign * dz) % 4 * 2 + (me % 2 + dc) % 2


def score_tile(query, keys, marks, scores, tops):
    running = None
    for start in range(0, TOKENS, CHUNK):
        first = start // TILE
        key = keys[pl.ds(first, CHUNK // TILE)].reshape(CHUNK, HD)
        key = jnp.concatenate([key, marks[pl.ds(start, CHUNK), :]], axis=1)
        part = lax.dot_general(query, key, NT, preferred_element_type=F32)
        scores[:, pl.ds(start, CHUNK)] = part
        for lane in range(0, CHUNK, 128):
            piece = part[:, lane : lane + 128]
            running = piece if running is None else jnp.maximum(running, piece)
    top = jnp.max(running, axis=1, keepdims=True)
    tops[...] = jnp.broadcast_to(top, tops.shape)


def value_tile(scores, tops, values):
    top = jnp.concatenate([tops[...]] * (CHUNK // 128), axis=1)
    total = None
    ones = jnp.ones((CHUNK, HD), BF16)
    for start in range(0, TOKENS, CHUNK):
        first = start // TILE
        value = values[pl.ds(first, CHUNK // TILE)].reshape(CHUNK, HD)
        value = jnp.concatenate([value, ones], axis=1)
        weights = jnp.exp2((scores[:, pl.ds(start, CHUNK)] - top) * EXPONENT).astype(BF16)
        part = jnp.dot(weights, value, preferred_element_type=F32)
        total = part if total is None else total + part
    return (total[:, :HD] / total[:, HD:]).astype(BF16)


def kernel(
    q_hbm, k_hbm, v_hbm, kind, smask, tmask,
    out,
    q_in, k_in, v_in, q_send, k_send, v_send, qt_send, kt_send, vt_send,
    q_got, k_got, v_got, o_send, o_got, marks,
    scores0, scores1, tops0, tops1, place, order,
    load_sem, send_sem, kv_sem, q_sem, o_sem, osend_sem,
):
    group = lax.axis_index("frame")
    band = lax.axis_index("band")

    barrier = pltpu.get_barrier_semaphore()
    for i in range(1, 16):
        pl.semaphore_signal(barrier, inc=1, device_id={"band": band_at(band, i, 1)}, device_id_type=MESH)
    for i in range(1, 8):
        pl.semaphore_signal(barrier, inc=1, device_id={"frame": frame_at(group, i, 1)}, device_id_type=MESH)

    loads = []
    for i, (source, target) in enumerate(((k_hbm, k_in), (v_hbm, v_in), (q_hbm, q_in))):
        for h in range(HEADS):
            pltpu.make_async_copy(source.at[:, :, pl.ds(h * HD, HD)], target.at[h], load_sem.at[i]).start()
        loads.append(pltpu.make_async_copy(target, target, load_sem.at[i]))

    before = jnp.int32(0)
    counts = []
    for h in range(HEADS):
        here = kind[h]
        place[h] = jnp.minimum(here * before + (1 - here) * (SPATIAL + h - before), HEADS - 1)
        before = before + here
        counts.append(before)

    def fill(slot, carry):
        spatial, temporal = jnp.int32(0), jnp.int32(0)
        for h in range(HEADS):
            spatial = spatial + (counts[h] <= slot).astype(jnp.int32)
            temporal = temporal + (h + 1 - counts[h] <= slot).astype(jnp.int32)
        order[slot] = jnp.minimum(spatial, HEADS - 1)

        @pl.when(slot < TEMPORAL)
        def _():
            order[SPATIAL + slot] = jnp.minimum(temporal, HEADS - 1)

        return carry

    lax.fori_loop(0, SPATIAL, fill, 0)

    lane = lax.broadcasted_iota(jnp.int32, (TILE, 128), 1)
    for t in range(TILES):
        marks[pl.ds(t * TILE, TILE), :] = jnp.where(lane == t, 1.0, 0.0).astype(BF16)

    lane = lax.broadcasted_iota(jnp.int32, (PAD, 128), 1)

    def mask_rows(read):
        rows = jnp.zeros((PAD, 128), F32)
        for t in range(TILES):
            rows = jnp.where(lane == t, (1 - read(t)).astype(F32) * NEGATIVE, rows)
        return rows.astype(BF16)

    spatial_rows = [mask_rows(lambda t, f=f: smask[f, 0, t]) for f in range(2)]
    temporal_rows = [mask_rows(lambda t, f=f: tmask[0, f, t]) for f in range(2)]

    def head(ref, f, slot):
        return ref[order[slot], f]

    def send_spatial(which, f, kind_index):
        source, staged, got = which
        query = staged is q_send
        for i in range(16):
            dest = band_at(band, i, 1)
            block = head(source, f, dest)
            if i == 0:
                got[f, band, pl.ds(0, TILE), :] = block
                if query:
                    got[f, band, pl.ds(TILE, PAD), :] = spatial_rows[f]
                continue
            staged[f, i, pl.ds(0, TILE), :] = block
            if query:
                staged[f, i, pl.ds(TILE, PAD), :] = spatial_rows[f]
            pltpu.make_async_remote_copy(
                src_ref=staged.at[f, i],
                dst_ref=got.at[f, band],
                send_sem=send_sem.at[kind_index, f],
                recv_sem=q_sem.at[f, i] if query else kv_sem.at[kind_index, f],
                device_id={"band": dest},
                device_id_type=MESH,
            ).start()

    def send_temporal(which, kind_index):
        source, staged, got = which
        query = staged is qt_send
        for i in range(8):
            dest = frame_at(group, i, 1)
            for f in range(2):
                block = head(source, f, SPATIAL + dest)
                if i == 0:
                    got[2, 2 * group + f, pl.ds(0, TILE), :] = block
                    if query:
                        got[2, 2 * group + f, pl.ds(TILE, PAD), :] = temporal_rows[f]
                else:
                    staged[i, f, pl.ds(0, TILE), :] = block
                    if query:
                        staged[i, f, pl.ds(TILE, PAD), :] = temporal_rows[f]
            if i > 0:
                pltpu.make_async_remote_copy(
                    src_ref=staged.at[i],
                    dst_ref=got.at[2, pl.ds(2 * group, 2)],
                    send_sem=send_sem.at[kind_index, 2],
                    recv_sem=q_sem.at[2, i] if query else kv_sem.at[kind_index, 2],
                    device_id={"frame": dest},
                    device_id_type=MESH,
                ).start()

    spatial_k, spatial_v, spatial_q = (k_in, k_send, k_got), (v_in, v_send, v_got), (q_in, q_send, q_got)
    temporal_k, temporal_v, temporal_q = (k_in, kt_send, k_got), (v_in, vt_send, v_got), (q_in, qt_send, q_got)

    loads[0].wait()
    pl.semaphore_wait(barrier, 22)
    send_spatial(spatial_k, 0, 0)
    send_temporal(temporal_k, 0)
    loads[1].wait()
    send_spatial(spatial_v, 0, 1)
    send_temporal(temporal_v, 1)
    loads[2].wait()
    send_spatial(spatial_q, 0, 2)
    send_temporal(temporal_q, 2)
    send_spatial(spatial_k, 1, 0)
    send_spatial(spatial_v, 1, 1)
    send_spatial(spatial_q, 1, 2)

    def wait_bytes(ref, sem):
        pltpu.make_async_copy(ref, ref, sem).wait()

    def wait_keys(u):
        many = 15 if u < 2 else 14
        wait_bytes(k_got.at[u, pl.ds(0, many)], kv_sem.at[0, u])
        wait_bytes(v_got.at[u, pl.ds(0, many)], kv_sem.at[1, u])

    def tiles_of(u, step):
        if u < 2:
            return band_at(band, 2 * step, -1), band_at(band, 2 * step + 1, -1)
        source = frame_at(group, step, -1)
        return 2 * source, 2 * source + 1

    def wait_query(u, step):
        if u < 2:

            @pl.when(step > 0)
            def _():
                wait_bytes(q_got.at[u, 0], q_sem.at[u, 2 * step])

            wait_bytes(q_got.at[u, 0], q_sem.at[u, 2 * step + 1])
        else:

            @pl.when(step > 0)
            def _():
                wait_bytes(q_got.at[u, pl.ds(0, 2)], q_sem.at[u, step])

    def run_scores(u, step, scores, tops):
        rows = []
        for t in tiles_of(u, step):
            bias = jnp.concatenate([q_got[u, t, pl.ds(TILE, PAD), :]] * (TILE // PAD), axis=0)
            rows.append(jnp.concatenate([q_got[u, t, pl.ds(0, TILE), :], bias], axis=1))
        score_tile(jnp.concatenate(rows, axis=0), k_got.at[u], marks, scores, tops)

    def run_values(u, step, scores, tops):
        result = value_tile(scores, tops, v_got.at[u])
        first, second = tiles_of(u, step)
        o_send[u, first] = result[:TILE]
        o_send[u, second] = result[TILE:]
        if u < 2:
            for t, guarded in ((first, True), (second, False)):
                copy = pltpu.make_async_remote_copy(
                    src_ref=o_send.at[u, t],
                    dst_ref=o_got.at[band, u],
                    send_sem=osend_sem.at[u],
                    recv_sem=o_sem.at[u],
                    device_id={"band": t},
                    device_id_type=MESH,
                )
                if guarded:
                    pl.when(step > 0)(copy.start)
                else:
                    copy.start()
        else:
            copy = pltpu.make_async_remote_copy(
                src_ref=o_send.at[2, pl.ds(first, 2)],
                dst_ref=o_got.at[SPATIAL + group],
                send_sem=osend_sem.at[u],
                recv_sem=o_sem.at[u],
                device_id={"frame": first // 2},
                device_id_type=MESH,
            )
            pl.when(step > 0)(copy.start)

    def run_unit(u):
        wait_keys(u)
        wait_query(u, 0)
        run_scores(u, 0, scores0, tops0)

        def body(i, carry):
            wait_query(u, 2 * i + 1)
            run_scores(u, 2 * i + 1, scores1, tops1)
            run_values(u, 2 * i, scores0, tops0)

            @pl.when(i < 3)
            def _():
                wait_query(u, 2 * i + 2)

            run_scores(u, jnp.minimum(2 * i + 2, 7), scores0, tops0)
            run_values(u, 2 * i + 1, scores1, tops1)
            return carry

        lax.fori_loop(0, 4, body, 0)

    run_unit(0)
    run_unit(2)
    run_unit(1)

    for f in range(2):
        o_got[band, f] = o_send[f, band]
        o_got[SPATIAL + group, f] = o_send[2, 2 * group + f]

    for f in range(2):
        wait_bytes(k_send.at[f, pl.ds(1, 15)], send_sem.at[0, f])
        wait_bytes(v_send.at[f, pl.ds(1, 15)], send_sem.at[1, f])
        wait_bytes(q_send.at[f, pl.ds(1, 15)], send_sem.at[2, f])
    wait_bytes(kt_send.at[pl.ds(1, 7)], send_sem.at[0, 2])
    wait_bytes(vt_send.at[pl.ds(1, 7)], send_sem.at[1, 2])
    wait_bytes(qt_send.at[pl.ds(1, 7)], send_sem.at[2, 2])
    for u, many in ((0, 15), (1, 15), (2, 14)):
        wait_bytes(o_send.at[u, pl.ds(0, many)], osend_sem.at[u])
    for u, many in ((0, 15), (1, 15), (2, 14)):
        wait_bytes(o_send.at[u, pl.ds(0, many)], o_sem.at[u])

    for h in range(HEADS):
        for f in range(2):
            out[f, :, pl.ds(h * HD, HD)] = o_got[place[h], f]


def body(queries, keys, values, head_kind, spatial_mask, temporal_mask):
    vmem, sem = pltpu.VMEM, pltpu.SemaphoreType.DMA
    hbm = pl.BlockSpec(memory_space=pl.ANY)
    smem = pl.BlockSpec(memory_space=pltpu.SMEM)
    return pl.pallas_call(
        kernel,
        out_shape=jax.ShapeDtypeStruct(queries.shape, BF16),
        in_specs=[hbm, hbm, hbm, smem, smem, smem],
        out_specs=pl.BlockSpec(memory_space=pltpu.VMEM),
        scratch_shapes=[
            vmem((HEADS, 2, TILE, HD), BF16), vmem((HEADS, 2, TILE, HD), BF16), vmem((HEADS, 2, TILE, HD), BF16),
            vmem((2, 16, QROWS, HD), BF16), vmem((2, 16, TILE, HD), BF16), vmem((2, 16, TILE, HD), BF16),
            vmem((8, 2, QROWS, HD), BF16), vmem((8, 2, TILE, HD), BF16), vmem((8, 2, TILE, HD), BF16),
            vmem((3, TILES, QROWS, HD), BF16), vmem((3, TILES, TILE, HD), BF16), vmem((3, TILES, TILE, HD), BF16),
            vmem((3, TILES, TILE, HD), BF16), vmem((HEADS, 2, TILE, HD), BF16),
            vmem((TOKENS, 128), BF16),
            vmem((256, TOKENS), F32), vmem((256, TOKENS), F32), vmem((256, 128), F32), vmem((256, 128), F32),
            pltpu.SMEM((HEADS,), jnp.int32), pltpu.SMEM((HEADS,), jnp.int32),
            sem((3,)), sem((3, 3)), sem((2, 3)), sem((3, 16)), sem((3,)), sem((3,)),
        ],
        compiler_params=pltpu.CompilerParams(
            collective_id=0, has_side_effects=True, vmem_limit_bytes=48 * 2**20
        ),
        cost_estimate=pl.CostEstimate(flops=6442450944, bytes_accessed=6291456, transcendentals=12582912),
    )(queries, keys, values, head_kind, spatial_mask, temporal_mask)


def solution(mesh):
    return jax.shard_map(
        body,
        mesh=mesh,
        in_specs=(
            P("frame", "band", None),
            P("frame", "band", None),
            P("frame", "band", None),
            P(),
            P("frame", "band", None),
            P("band", "frame", None),
        ),
        out_specs=P("frame", "band", None),
        check_vma=False,
    )
```

```python
import functools
import math

import jax
import jax.numpy as jnp
from jax import lax
from jax.experimental import pallas as pl
from jax.experimental.pallas import tpu as pltpu
from jax.sharding import PartitionSpec as P

MESH = pl.DeviceIdType.MESH
HD = 128
HEADS = 24
SPATIAL = 16
TEMPORAL = HEADS - SPATIAL
TILE = 128
TILES = 16
TOKENS = TILES * TILE
NEGATIVE = -1e30
EXPONENT = math.log2(math.e) / math.sqrt(HD)
CHUNK = 512
NT = (((1,), (1,)), ((), ()))
BF16 = jnp.bfloat16
F32 = jnp.float32

BAND_STEPS = (
    (0, 0), (1, 0), (0, 3), (3, 0), (0, 1), (2, 0), (0, 2), (1, 1),
    (3, 3), (1, 3), (3, 1), (2, 1), (1, 2), (2, 3), (3, 2), (2, 2),
)
FRAME_STEPS = ((0, 0), (0, 1), (1, 0), (3, 0), (1, 1), (3, 1), (2, 0), (2, 1))


def pick(table, index):
    if isinstance(index, int):
        return table[index]
    value = jnp.int32(table[0])
    for place in range(1, len(table)):
        value = jnp.where(index == place, jnp.int32(table[place]), value)
    return value


def when(condition, action):
    if isinstance(condition, bool):
        if condition:
            action()
    else:
        pl.when(condition)(action)


def band_at(me, index, sign):
    dx = pick([s[0] for s in BAND_STEPS], index)
    dy = pick([s[1] for s in BAND_STEPS], index)
    return (me // 4 + 4 + sign * dx) % 4 * 4 + (me % 4 + 4 + sign * dy) % 4


def frame_at(me, index, sign):
    dz = pick([s[0] for s in FRAME_STEPS], index)
    dc = pick([s[1] for s in FRAME_STEPS], index)
    return (me // 2 + 4 + sign * dz) % 4 * 2 + (me % 2 + dc) % 2


def score_tile(query, keys, marks, scores, tops):
    running = None
    for start in range(0, TOKENS, CHUNK):
        first = start // TILE
        key = keys[pl.ds(first, CHUNK // TILE), 0].reshape(CHUNK, HD)
        key = jnp.concatenate([key, marks[pl.ds(start, CHUNK), :]], axis=1)
        part = lax.dot_general(query, key, NT, preferred_element_type=F32)
        scores[:, pl.ds(start, CHUNK)] = part
        for lane in range(0, CHUNK, 128):
            piece = part[:, lane : lane + 128]
            running = piece if running is None else jnp.maximum(running, piece)
    top = jnp.max(running, axis=1, keepdims=True)
    tops[...] = jnp.broadcast_to(top, tops.shape)


def value_tile(scores, tops, values):
    top = jnp.concatenate([tops[...]] * (CHUNK // 128), axis=1)
    total = None
    ones = jnp.ones((CHUNK, HD), BF16)
    for start in range(0, TOKENS, CHUNK):
        first = start // TILE
        value = values[pl.ds(first, CHUNK // TILE), 1].reshape(CHUNK, HD)
        value = jnp.concatenate([value, ones], axis=1)
        weights = jnp.exp2((scores[:, pl.ds(start, CHUNK)] - top) * EXPONENT).astype(BF16)
        part = jnp.dot(weights, value, preferred_element_type=F32)
        total = part if total is None else total + part
    return (total[:, :HD] / total[:, HD:]).astype(BF16)


def kernel(
    q_hbm, k_hbm, v_hbm, ints_hbm,
    out,
    q_in, k_in, v_in, q_send, kv_send, qt_send, kvt_send, row_send,
    q_got, kv_got, row_got, o_send, o_got, marks,
    scores0, scores1, tops0, tops1, ints, place, order,
    load_sem, send_sem, kv_sem, row_sem, q_sem, o_sem, osend_sem, groups_in, all_in,
):
    group = lax.axis_index("frame")
    band = lax.axis_index("band")

    barrier = pltpu.get_barrier_semaphore()
    for i in range(1, 16):
        pl.semaphore_signal(barrier, inc=1, device_id={"band": band_at(band, i, 1)}, device_id_type=MESH)

    def greet_groups(sem):
        for i in range(1, 8):
            pl.semaphore_signal(sem, inc=1, device_id={"frame": frame_at(group, i, 1)}, device_id_type=MESH)

    pl.when(band == 0)(lambda: greet_groups(barrier))

    small = pltpu.make_async_copy(ints_hbm, ints, load_sem.at[3])
    small.start()
    def load(i, source, target):
        for h in range(HEADS):
            pltpu.make_async_copy(source.at[:, :, pl.ds(h * HD, HD)], target.at[h], load_sem.at[i]).start()
        return pltpu.make_async_copy(target, target, load_sem.at[i])

    k_load = load(0, k_hbm, k_in)
    v_load = load(1, v_hbm, v_in)
    small.wait()
    before = jnp.int32(0)
    counts = []
    for h in range(HEADS):
        here = ints[1, 2, h]
        place[h] = jnp.minimum(here * before + (1 - here) * (SPATIAL + h - before), HEADS - 1)
        before = before + here
        counts.append(before)

    def fill(slot, carry):
        spatial, temporal = jnp.int32(0), jnp.int32(0)
        for h in range(HEADS):
            spatial = spatial + (counts[h] <= slot).astype(jnp.int32)
            temporal = temporal + (h + 1 - counts[h] <= slot).astype(jnp.int32)
        order[slot] = jnp.minimum(spatial, HEADS - 1)

        @pl.when(slot < TEMPORAL)
        def _():
            order[SPATIAL + slot] = jnp.minimum(temporal, HEADS - 1)

        return carry

    lax.fori_loop(0, SPATIAL, fill, 0)

    lane = lax.broadcasted_iota(jnp.int32, (1, 128), 1)
    for kind in range(2):
        for f in range(2):
            row = jnp.zeros((1, 128), F32)
            for t in range(TILES):
                row = jnp.where(lane == t, (1 - ints[f, kind, t]).astype(F32) * NEGATIVE, row)
            row_send[kind, f] = row
            if kind == 0:
                row_got[f, band] = row
            else:
                row_got[2, 2 * group + f] = row

    def head(ref, f, slot):
        return ref[order[slot], f]

    def send(source, target, device, sent, got):
        pltpu.make_async_remote_copy(
            src_ref=source,
            dst_ref=target,
            send_sem=sent,
            recv_sem=got,
            device_id=device,
            device_id_type=MESH,
        ).start()

    def send_rows(kind):
        for i in range(1, 16 - 8 * kind):
            if kind == 0:
                target, device = row_got.at[pl.ds(0, 2), band], {"band": band_at(band, i, 1)}
            else:
                target, device = row_got.at[2, pl.ds(2 * group, 2)], {"frame": frame_at(group, i, 1)}
            send(row_send.at[kind], target, device, send_sem.at[2, kind], row_sem.at[kind])

    def keep_own(f):
        kv_got[f, band, 0] = head(k_in, f, band)
        kv_got[f, band, 1] = head(v_in, f, band)
        q_got[f, band] = head(q_in, f, band)
        kv_got[2, 2 * group + f, 0] = head(k_in, f, SPATIAL + group)
        kv_got[2, 2 * group + f, 1] = head(v_in, f, SPATIAL + group)
        q_got[2, 2 * group + f] = head(q_in, f, SPATIAL + group)

    def send_keys(f, places):
        for i in places:
            dest = band_at(band, i, 1)
            kv_send[f, i, 0] = head(k_in, f, dest)
            kv_send[f, i, 1] = head(v_in, f, dest)
            send(kv_send.at[f, i], kv_got.at[f, band], {"band": dest}, send_sem.at[0, f], kv_sem.at[f])

    def send_queries(f, places):
        for i in places:
            dest = band_at(band, i, 1)
            q_send[f, i] = head(q_in, f, dest)
            send(q_send.at[f, i], q_got.at[f, band], {"band": dest}, send_sem.at[1, f], q_sem.at[f, i])

    def send_temporal():
        for i in range(1, 8):
            dest = frame_at(group, i, 1)
            for f in range(2):
                kvt_send[i, f, 0] = head(k_in, f, SPATIAL + dest)
                kvt_send[i, f, 1] = head(v_in, f, SPATIAL + dest)
            send(kvt_send.at[i], kv_got.at[2, pl.ds(2 * group, 2)], {"frame": dest}, send_sem.at[0, 2], kv_sem.at[2])
        for i in range(1, 8):
            dest = frame_at(group, i, 1)
            for f in range(2):
                qt_send[i, f] = head(q_in, f, SPATIAL + dest)
            send(qt_send.at[i], q_got.at[2, pl.ds(2 * group, 2)], {"frame": dest}, send_sem.at[1, 2], q_sem.at[2, i])

    everyone = range(1, 16)
    q_load = load(2, q_hbm, q_in)
    k_load.wait()
    v_load.wait()
    pl.when(band > 0)(lambda: pl.semaphore_wait(barrier, 15))

    @pl.when(band == 0)
    def _():
        pl.semaphore_wait(barrier, 22)
        greet_groups(groups_in)

    send_keys(0, everyone)
    send_rows(0)
    q_load.wait()
    send_queries(0, everyone)

    @pl.when(band == 0)
    def _():
        pl.semaphore_wait(groups_in, 7)
        for i in range(1, 16):
            pl.semaphore_signal(all_in, inc=1, device_id={"band": band_at(band, i, 1)}, device_id_type=MESH)

    pl.when(band > 0)(lambda: pl.semaphore_wait(all_in, 1))
    send_temporal()
    send_rows(1)
    send_keys(1, everyone)
    send_queries(1, everyone)
    keep_own(0)
    keep_own(1)

    lane = lax.broadcasted_iota(jnp.int32, (TILE, 128), 1)
    for t in range(TILES):
        marks[pl.ds(t * TILE, TILE), :] = jnp.where(lane == t, 1.0, 0.0).astype(BF16)

    def wait_bytes(ref, sem):
        pltpu.make_async_copy(ref, ref, sem).wait()

    def wait_keys(u):
        many = 15 if u < 2 else 14
        wait_bytes(kv_got.at[u, pl.ds(0, many)], kv_sem.at[u])

    def tiles_of(u, step):
        if u < 2:
            return band_at(band, 2 * step, -1), band_at(band, 2 * step + 1, -1)
        source = frame_at(group, step, -1)
        return 2 * source, 2 * source + 1

    def wait_query(u, step):
        if u < 2:

            def first():
                wait_bytes(q_got.at[u, 0], q_sem.at[u, 2 * step])

            when(step > 0, first)

            wait_bytes(q_got.at[u, 0], q_sem.at[u, 2 * step + 1])
        else:

            when(step > 0, lambda: wait_bytes(q_got.at[u, pl.ds(0, 2)], q_sem.at[u, step]))

    def run_scores(u, step, scores, tops):
        rows = []
        for t in tiles_of(u, step):
            bias = jnp.broadcast_to(row_got[u, t], (TILE, 128)).astype(BF16)
            rows.append(jnp.concatenate([q_got[u, t], bias], axis=1))
        score_tile(jnp.concatenate(rows, axis=0), kv_got.at[u], marks, scores, tops)

    def run_values(u, step, scores, tops):
        result = value_tile(scores, tops, kv_got.at[u])
        first, second = tiles_of(u, step)
        o_send[u, first] = result[:TILE]
        o_send[u, second] = result[TILE:]
        if u == 0:
            return
        if u < 2:
            for t, guarded in ((first, True), (second, False)):
                copy = pltpu.make_async_remote_copy(
                    src_ref=o_send.at[u, t],
                    dst_ref=o_got.at[band, u],
                    send_sem=osend_sem.at[u],
                    recv_sem=o_sem.at[u],
                    device_id={"band": t},
                    device_id_type=MESH,
                )
                if guarded:
                    when(step > 0, copy.start)
                else:
                    copy.start()
        else:
            copy = pltpu.make_async_remote_copy(
                src_ref=o_send.at[2, pl.ds(first, 2)],
                dst_ref=o_got.at[SPATIAL + group],
                send_sem=osend_sem.at[u],
                recv_sem=o_sem.at[u],
                device_id={"frame": first // 2},
                device_id_type=MESH,
            )
            when(step > 0, copy.start)

    def run_unit(u):
        wait_keys(u)
        if u == 1:
            for i in range(1, 16):
                t = band_at(band, i, -1)
                pltpu.make_async_remote_copy(
                    src_ref=o_send.at[0, t],
                    dst_ref=o_got.at[band, 0],
                    send_sem=osend_sem.at[0],
                    recv_sem=o_sem.at[0],
                    device_id={"band": t},
                    device_id_type=MESH,
                ).start()
        wait_query(u, 0)
        run_scores(u, 0, scores0, tops0)

        def body(i, carry):
            wait_query(u, 2 * i + 1)
            run_scores(u, 2 * i + 1, scores1, tops1)
            run_values(u, 2 * i, scores0, tops0)

            wait_query(u, 2 * i + 2)
            run_scores(u, 2 * i + 2, scores0, tops0)
            run_values(u, 2 * i + 1, scores1, tops1)
            return carry

        lax.fori_loop(0, 3, body, 0)
        wait_query(u, 7)
        run_scores(u, 7, scores1, tops1)
        run_values(u, 6, scores0, tops0)
        run_values(u, 7, scores1, tops1)

    wait_bytes(row_got.at[pl.ds(0, 2), pl.ds(0, 15)], row_sem.at[0])
    run_unit(0)
    wait_bytes(row_got.at[2, pl.ds(0, 14)], row_sem.at[1])
    run_unit(2)
    run_unit(1)

    for f in range(2):
        o_got[band, f] = o_send[f, band]
        o_got[SPATIAL + group, f] = o_send[2, 2 * group + f]

    for f in range(2):
        wait_bytes(kv_send.at[f, pl.ds(1, 15)], send_sem.at[0, f])
        wait_bytes(q_send.at[f, pl.ds(1, 15)], send_sem.at[1, f])
    wait_bytes(kvt_send.at[pl.ds(1, 7)], send_sem.at[0, 2])
    wait_bytes(qt_send.at[pl.ds(1, 7)], send_sem.at[1, 2])
    wait_bytes(row_got.at[pl.ds(0, 2), pl.ds(0, 15)], send_sem.at[2, 0])
    wait_bytes(row_got.at[2, pl.ds(0, 14)], send_sem.at[2, 1])
    for u, many in ((0, 15), (1, 15), (2, 14)):
        wait_bytes(o_send.at[u, pl.ds(0, many)], osend_sem.at[u])
    for u, many in ((0, 15), (1, 15), (2, 14)):
        wait_bytes(o_send.at[u, pl.ds(0, many)], o_sem.at[u])

    for h in range(HEADS):
        for f in range(2):
            out[f, :, pl.ds(h * HD, HD)] = o_got[place[h], f]


def body(queries, keys, values, head_kind, spatial_mask, temporal_mask):
    vmem, sem = pltpu.VMEM, pltpu.SemaphoreType.DMA
    hbm = pl.BlockSpec(memory_space=pltpu.HBM)
    wide = HEADS - TILES
    ints = (
        jnp.pad(spatial_mask, ((0, 0), (0, 2), (0, wide)))
        + jnp.pad(temporal_mask.transpose(1, 0, 2), ((0, 0), (1, 1), (0, wide)))
        + jnp.pad(head_kind.reshape(1, 1, HEADS), ((1, 0), (2, 0), (0, 0)))
    )
    return pl.pallas_call(
        kernel,
        out_shape=jax.ShapeDtypeStruct(queries.shape, BF16),
        in_specs=[hbm] * 4,
        out_specs=pl.BlockSpec(memory_space=pltpu.VMEM),
        scratch_shapes=[
            vmem((HEADS, 2, TILE, HD), BF16), vmem((HEADS, 2, TILE, HD), BF16), vmem((HEADS, 2, TILE, HD), BF16),
            vmem((2, 16, TILE, HD), BF16), vmem((2, 16, 2, TILE, HD), BF16),
            vmem((8, 2, TILE, HD), BF16), vmem((8, 2, 2, TILE, HD), BF16), vmem((2, 2, 1, 128), F32),
            vmem((3, TILES, TILE, HD), BF16), vmem((3, TILES, 2, TILE, HD), BF16), vmem((3, TILES, 1, 128), F32),
            vmem((3, TILES, TILE, HD), BF16), vmem((HEADS, 2, TILE, HD), BF16),
            vmem((TOKENS, 128), BF16),
            vmem((256, TOKENS), F32), vmem((256, TOKENS), F32), vmem((256, 128), F32), vmem((256, 128), F32),
            pltpu.SMEM((2, 3, HEADS), jnp.int32),
            pltpu.SMEM((HEADS,), jnp.int32), pltpu.SMEM((HEADS,), jnp.int32),
            sem((4,)), sem((3, 3)), sem((3,)), sem((2,)), sem((3, 16)), sem((3,)), sem((3,)),
            pltpu.SemaphoreType.REGULAR, pltpu.SemaphoreType.REGULAR,
        ],
        compiler_params=pltpu.CompilerParams(
            collective_id=0, has_side_effects=True, vmem_limit_bytes=52 * 2**20
        ),
        cost_estimate=pl.CostEstimate(flops=6442450944, bytes_accessed=6291456, transcendentals=12582912),
    )(queries, keys, values, ints)


def solution(mesh):
    return jax.shard_map(
        body,
        mesh=mesh,
        in_specs=(
            P("frame", "band", None),
            P("frame", "band", None),
            P("frame", "band", None),
            P(),
            P("frame", "band", None),
            P("band", "frame", None),
        ),
        out_specs=P("frame", "band", None),
        check_vma=False,
    )
```

```python
import functools
import math

import jax
import jax.numpy as jnp
from jax import lax
from jax.experimental import pallas as pl
from jax.experimental.pallas import tpu as pltpu
from jax.sharding import PartitionSpec as P

MESH = pl.DeviceIdType.MESH
HD = 128
HEADS = 24
SPATIAL = 16
TEMPORAL = HEADS - SPATIAL
TILE = 128
TILES = 16
TOKENS = TILES * TILE
NEGATIVE = -1e30
EXPONENT = math.log2(math.e) / math.sqrt(HD)
CHUNK = 512
NT = (((1,), (1,)), ((), ()))
BF16 = jnp.bfloat16
F32 = jnp.float32

BAND_STEPS = (
    (0, 0), (1, 0), (0, 3), (3, 0), (0, 1), (2, 0), (0, 2), (1, 1),
    (3, 3), (1, 3), (3, 1), (2, 1), (1, 2), (2, 3), (3, 2), (2, 2),
)
FRAME_STEPS = ((0, 0), (0, 1), (1, 0), (3, 0), (1, 1), (3, 1), (2, 0), (2, 1))


def pick(table, index):
    if isinstance(index, int):
        return table[index]
    value = jnp.int32(table[0])
    for place in range(1, len(table)):
        value = jnp.where(index == place, jnp.int32(table[place]), value)
    return value


def when(condition, action):
    if isinstance(condition, bool):
        if condition:
            action()
    else:
        pl.when(condition)(action)


def band_at(me, index, sign):
    dx = pick([s[0] for s in BAND_STEPS], index)
    dy = pick([s[1] for s in BAND_STEPS], index)
    return (me // 4 + 4 + sign * dx) % 4 * 4 + (me % 4 + 4 + sign * dy) % 4


def frame_at(me, index, sign):
    dz = pick([s[0] for s in FRAME_STEPS], index)
    dc = pick([s[1] for s in FRAME_STEPS], index)
    return (me // 2 + 4 + sign * dz) % 4 * 2 + (me % 2 + dc) % 2


def score_tile(query, keys, marks, scores, tops):
    running = None
    for start in range(0, TOKENS, CHUNK):
        first = start // TILE
        key = keys[pl.ds(first, CHUNK // TILE), 0].reshape(CHUNK, HD)
        key = jnp.concatenate([key, marks[pl.ds(start, CHUNK), :]], axis=1)
        part = lax.dot_general(query, key, NT, preferred_element_type=F32)
        scores[:, pl.ds(start, CHUNK)] = part
        for lane in range(0, CHUNK, 128):
            piece = part[:, lane : lane + 128]
            running = piece if running is None else jnp.maximum(running, piece)
    top = jnp.max(running, axis=1, keepdims=True)
    tops[...] = jnp.broadcast_to(top, tops.shape)


def value_tile(scores, tops, values):
    top = jnp.concatenate([tops[...]] * (CHUNK // 128), axis=1)
    total = None
    ones = jnp.ones((CHUNK, HD), BF16)
    for start in range(0, TOKENS, CHUNK):
        first = start // TILE
        value = values[pl.ds(first, CHUNK // TILE), 1].reshape(CHUNK, HD)
        value = jnp.concatenate([value, ones], axis=1)
        weights = jnp.exp2((scores[:, pl.ds(start, CHUNK)] - top) * EXPONENT).astype(BF16)
        part = jnp.dot(weights, value, preferred_element_type=F32)
        total = part if total is None else total + part
    return (total[:, :HD] / total[:, HD:]).astype(BF16)


def kernel(
    q_hbm, k_hbm, v_hbm, ints_hbm,
    out,
    q_in, k_in, v_in, q_send, kv_send, qt_send, kvt_send, row_send,
    q_got, kv_got, row_got, o_send, o_got, marks,
    scores0, scores1, tops0, tops1, ints, place, order,
    load_sem, send_sem, kv_sem, row_sem, q_sem, o_sem, osend_sem, groups_in, all_in,
):
    group = lax.axis_index("frame")
    band = lax.axis_index("band")

    barrier = pltpu.get_barrier_semaphore()
    for i in range(1, 16):
        pl.semaphore_signal(barrier, inc=1, device_id={"band": band_at(band, i, 1)}, device_id_type=MESH)

    leader = band % 4 == 0

    def greet_groups(sem):
        for i in range(1, 8):
            pl.semaphore_signal(sem, inc=1, device_id={"frame": frame_at(group, i, 1)}, device_id_type=MESH)

    pl.when(leader)(lambda: greet_groups(barrier))

    small = pltpu.make_async_copy(ints_hbm, ints, load_sem.at[3])
    small.start()
    def load(i, source, target):
        for h in range(HEADS):
            pltpu.make_async_copy(source.at[:, :, pl.ds(h * HD, HD)], target.at[h], load_sem.at[i]).start()
        return pltpu.make_async_copy(target, target, load_sem.at[i])

    k_load = load(0, k_hbm, k_in)
    v_load = load(1, v_hbm, v_in)
    small.wait()
    before = jnp.int32(0)
    counts = []
    for h in range(HEADS):
        here = ints[1, 2, h]
        place[h] = jnp.minimum(here * before + (1 - here) * (SPATIAL + h - before), HEADS - 1)
        before = before + here
        counts.append(before)

    def fill(slot, carry):
        spatial, temporal = jnp.int32(0), jnp.int32(0)
        for h in range(HEADS):
            spatial = spatial + (counts[h] <= slot).astype(jnp.int32)
            temporal = temporal + (h + 1 - counts[h] <= slot).astype(jnp.int32)
        order[slot] = jnp.minimum(spatial, HEADS - 1)

        @pl.when(slot < TEMPORAL)
        def _():
            order[SPATIAL + slot] = jnp.minimum(temporal, HEADS - 1)

        return carry

    lax.fori_loop(0, SPATIAL, fill, 0)

    lane = lax.broadcasted_iota(jnp.int32, (1, 128), 1)
    for kind in range(2):
        for f in range(2):
            row = jnp.zeros((1, 128), F32)
            for t in range(TILES):
                row = jnp.where(lane == t, (1 - ints[f, kind, t]).astype(F32) * NEGATIVE, row)
            row_send[kind, f] = row
            if kind == 0:
                row_got[f, band] = row
            else:
                row_got[2, 2 * group + f] = row

    def head(ref, f, slot):
        return ref[order[slot], f]

    def send(source, target, device, sent, got):
        pltpu.make_async_remote_copy(
            src_ref=source,
            dst_ref=target,
            send_sem=sent,
            recv_sem=got,
            device_id=device,
            device_id_type=MESH,
        ).start()

    def send_rows(kind):
        for i in range(1, 16 - 8 * kind):
            if kind == 0:
                target, device = row_got.at[pl.ds(0, 2), band], {"band": band_at(band, i, 1)}
            else:
                target, device = row_got.at[2, pl.ds(2 * group, 2)], {"frame": frame_at(group, i, 1)}
            send(row_send.at[kind], target, device, send_sem.at[2, kind], row_sem.at[kind])

    def keep_own(f):
        kv_got[f, band, 0] = head(k_in, f, band)
        kv_got[f, band, 1] = head(v_in, f, band)
        q_got[f, band] = head(q_in, f, band)
        kv_got[2, 2 * group + f, 0] = head(k_in, f, SPATIAL + group)
        kv_got[2, 2 * group + f, 1] = head(v_in, f, SPATIAL + group)
        q_got[2, 2 * group + f] = head(q_in, f, SPATIAL + group)

    def send_keys(f, places):
        for i in places:
            dest = band_at(band, i, 1)
            kv_send[f, i, 0] = head(k_in, f, dest)
            kv_send[f, i, 1] = head(v_in, f, dest)
            send(kv_send.at[f, i], kv_got.at[f, band], {"band": dest}, send_sem.at[0, f], kv_sem.at[f])

    def send_queries(f, places):
        for i in places:
            dest = band_at(band, i, 1)
            q_send[f, i] = head(q_in, f, dest)
            send(q_send.at[f, i], q_got.at[f, band], {"band": dest}, send_sem.at[1, f], q_sem.at[f, i])

    def send_temporal():
        for i in range(1, 8):
            dest = frame_at(group, i, 1)
            for f in range(2):
                kvt_send[i, f, 0] = head(k_in, f, SPATIAL + dest)
                kvt_send[i, f, 1] = head(v_in, f, SPATIAL + dest)
            send(kvt_send.at[i], kv_got.at[2, pl.ds(2 * group, 2)], {"frame": dest}, send_sem.at[0, 2], kv_sem.at[2])
        for i in range(1, 8):
            dest = frame_at(group, i, 1)
            for f in range(2):
                qt_send[i, f] = head(q_in, f, SPATIAL + dest)
            send(qt_send.at[i], q_got.at[2, pl.ds(2 * group, 2)], {"frame": dest}, send_sem.at[1, 2], q_sem.at[2, i])

    everyone = range(1, 16)
    q_load = load(2, q_hbm, q_in)
    k_load.wait()
    v_load.wait()
    pl.when(band % 4 > 0)(lambda: pl.semaphore_wait(barrier, 15))

    @pl.when(leader)
    def _():
        pl.semaphore_wait(barrier, 22)
        greet_groups(groups_in)

    send_keys(0, everyone)
    send_rows(0)
    q_load.wait()
    send_queries(0, everyone)

    @pl.when(leader)
    def _():
        pl.semaphore_wait(groups_in, 7)
        for i in range(1, 4):
            pl.semaphore_signal(all_in, inc=1, device_id={"band": band + i}, device_id_type=MESH)

    pl.when(band % 4 > 0)(lambda: pl.semaphore_wait(all_in, 1))
    send_temporal()
    send_rows(1)
    send_keys(1, everyone)
    send_queries(1, everyone)
    keep_own(0)
    keep_own(1)

    lane = lax.broadcasted_iota(jnp.int32, (TILE, 128), 1)
    for t in range(TILES):
        marks[pl.ds(t * TILE, TILE), :] = jnp.where(lane == t, 1.0, 0.0).astype(BF16)

    def wait_bytes(ref, sem):
        pltpu.make_async_copy(ref, ref, sem).wait()

    def wait_keys(u):
        many = 15 if u < 2 else 14
        wait_bytes(kv_got.at[u, pl.ds(0, many)], kv_sem.at[u])

    def tiles_of(u, step):
        if u < 2:
            return band_at(band, 2 * step, -1), band_at(band, 2 * step + 1, -1)
        source = frame_at(group, step, -1)
        return 2 * source, 2 * source + 1

    def wait_query(u, step):
        if u < 2:

            def first():
                wait_bytes(q_got.at[u, 0], q_sem.at[u, 2 * step])

            when(step > 0, first)

            wait_bytes(q_got.at[u, 0], q_sem.at[u, 2 * step + 1])
        else:

            when(step > 0, lambda: wait_bytes(q_got.at[u, pl.ds(0, 2)], q_sem.at[u, step]))

    def run_scores(u, step, scores, tops):
        rows = []
        for t in tiles_of(u, step):
            bias = jnp.broadcast_to(row_got[u, t], (TILE, 128)).astype(BF16)
            rows.append(jnp.concatenate([q_got[u, t], bias], axis=1))
        score_tile(jnp.concatenate(rows, axis=0), kv_got.at[u], marks, scores, tops)

    def run_values(u, step, scores, tops):
        result = value_tile(scores, tops, kv_got.at[u])
        first, second = tiles_of(u, step)
        o_send[u, first] = result[:TILE]
        o_send[u, second] = result[TILE:]
        if u == 0:
            return
        if u < 2:
            for t, guarded in ((first, True), (second, False)):
                copy = pltpu.make_async_remote_copy(
                    src_ref=o_send.at[u, t],
                    dst_ref=o_got.at[band, u],
                    send_sem=osend_sem.at[u],
                    recv_sem=o_sem.at[u],
                    device_id={"band": t},
                    device_id_type=MESH,
                )
                if guarded:
                    when(step > 0, copy.start)
                else:
                    copy.start()
        else:
            copy = pltpu.make_async_remote_copy(
                src_ref=o_send.at[2, pl.ds(first, 2)],
                dst_ref=o_got.at[SPATIAL + group],
                send_sem=osend_sem.at[u],
                recv_sem=o_sem.at[u],
                device_id={"frame": first // 2},
                device_id_type=MESH,
            )
            when(step > 0, copy.start)

    def run_unit(u):
        wait_keys(u)
        if u == 1:
            for i in range(1, 16):
                t = band_at(band, i, -1)
                pltpu.make_async_remote_copy(
                    src_ref=o_send.at[0, t],
                    dst_ref=o_got.at[band, 0],
                    send_sem=osend_sem.at[0],
                    recv_sem=o_sem.at[0],
                    device_id={"band": t},
                    device_id_type=MESH,
                ).start()
        wait_query(u, 0)
        run_scores(u, 0, scores0, tops0)

        def body(i, carry):
            wait_query(u, 2 * i + 1)
            run_scores(u, 2 * i + 1, scores1, tops1)
            run_values(u, 2 * i, scores0, tops0)

            wait_query(u, 2 * i + 2)
            run_scores(u, 2 * i + 2, scores0, tops0)
            run_values(u, 2 * i + 1, scores1, tops1)
            return carry

        lax.fori_loop(0, 3, body, 0)
        wait_query(u, 7)
        run_scores(u, 7, scores1, tops1)
        run_values(u, 6, scores0, tops0)
        run_values(u, 7, scores1, tops1)

    wait_bytes(row_got.at[pl.ds(0, 2), pl.ds(0, 15)], row_sem.at[0])
    run_unit(0)
    wait_bytes(row_got.at[2, pl.ds(0, 14)], row_sem.at[1])
    run_unit(2)
    run_unit(1)

    for f in range(2):
        o_got[band, f] = o_send[f, band]
        o_got[SPATIAL + group, f] = o_send[2, 2 * group + f]

    for f in range(2):
        wait_bytes(kv_send.at[f, pl.ds(1, 15)], send_sem.at[0, f])
        wait_bytes(q_send.at[f, pl.ds(1, 15)], send_sem.at[1, f])
    wait_bytes(kvt_send.at[pl.ds(1, 7)], send_sem.at[0, 2])
    wait_bytes(qt_send.at[pl.ds(1, 7)], send_sem.at[1, 2])
    wait_bytes(row_got.at[pl.ds(0, 2), pl.ds(0, 15)], send_sem.at[2, 0])
    wait_bytes(row_got.at[2, pl.ds(0, 14)], send_sem.at[2, 1])
    for u, many in ((0, 15), (1, 15), (2, 14)):
        wait_bytes(o_send.at[u, pl.ds(0, many)], osend_sem.at[u])
    for u, many in ((0, 15), (1, 15), (2, 14)):
        wait_bytes(o_send.at[u, pl.ds(0, many)], o_sem.at[u])

    for h in range(HEADS):
        for f in range(2):
            out[f, :, pl.ds(h * HD, HD)] = o_got[place[h], f]


def body(queries, keys, values, head_kind, spatial_mask, temporal_mask):
    vmem, sem = pltpu.VMEM, pltpu.SemaphoreType.DMA
    hbm = pl.BlockSpec(memory_space=pltpu.HBM)
    wide = HEADS - TILES
    ints = (
        jnp.pad(spatial_mask, ((0, 0), (0, 2), (0, wide)))
        + jnp.pad(temporal_mask.transpose(1, 0, 2), ((0, 0), (1, 1), (0, wide)))
        + jnp.pad(head_kind.reshape(1, 1, HEADS), ((1, 0), (2, 0), (0, 0)))
    )
    return pl.pallas_call(
        kernel,
        out_shape=jax.ShapeDtypeStruct(queries.shape, BF16),
        in_specs=[hbm] * 4,
        out_specs=pl.BlockSpec(memory_space=pltpu.VMEM),
        scratch_shapes=[
            vmem((HEADS, 2, TILE, HD), BF16), vmem((HEADS, 2, TILE, HD), BF16), vmem((HEADS, 2, TILE, HD), BF16),
            vmem((2, 16, TILE, HD), BF16), vmem((2, 16, 2, TILE, HD), BF16),
            vmem((8, 2, TILE, HD), BF16), vmem((8, 2, 2, TILE, HD), BF16), vmem((2, 2, 1, 128), F32),
            vmem((3, TILES, TILE, HD), BF16), vmem((3, TILES, 2, TILE, HD), BF16), vmem((3, TILES, 1, 128), F32),
            vmem((3, TILES, TILE, HD), BF16), vmem((HEADS, 2, TILE, HD), BF16),
            vmem((TOKENS, 128), BF16),
            vmem((256, TOKENS), F32), vmem((256, TOKENS), F32), vmem((256, 128), F32), vmem((256, 128), F32),
            pltpu.SMEM((2, 3, HEADS), jnp.int32),
            pltpu.SMEM((HEADS,), jnp.int32), pltpu.SMEM((HEADS,), jnp.int32),
            sem((4,)), sem((3, 3)), sem((3,)), sem((2,)), sem((3, 16)), sem((3,)), sem((3,)),
            pltpu.SemaphoreType.REGULAR, pltpu.SemaphoreType.REGULAR,
        ],
        compiler_params=pltpu.CompilerParams(
            collective_id=0, has_side_effects=True, vmem_limit_bytes=52 * 2**20
        ),
        cost_estimate=pl.CostEstimate(flops=6442450944, bytes_accessed=6291456, transcendentals=12582912),
    )(queries, keys, values, ints)


def solution(mesh):
    return jax.shard_map(
        body,
        mesh=mesh,
        in_specs=(
            P("frame", "band", None),
            P("frame", "band", None),
            P("frame", "band", None),
            P(),
            P("frame", "band", None),
            P("band", "frame", None),
        ),
        out_specs=P("frame", "band", None),
        check_vma=False,
    )
```

```python
import functools
import math

import jax
import jax.numpy as jnp
from jax import lax
from jax.experimental import pallas as pl
from jax.experimental.pallas import tpu as pltpu
from jax.sharding import PartitionSpec as P

MESH = pl.DeviceIdType.MESH
HD = 128
HEADS = 24
SPATIAL = 16
TEMPORAL = HEADS - SPATIAL
TILE = 128
TILES = 16
TOKENS = TILES * TILE
NEGATIVE = -1e30
EXPONENT = math.log2(math.e) / math.sqrt(HD)
CHUNK = 512
NT = (((1,), (1,)), ((), ()))
BF16 = jnp.bfloat16
F32 = jnp.float32

BAND_STEPS = (
    (0, 0), (1, 0), (0, 3), (3, 0), (0, 1), (2, 0), (0, 2), (1, 1),
    (3, 3), (1, 3), (3, 1), (2, 1), (1, 2), (2, 3), (3, 2), (2, 2),
)
FRAME_STEPS = ((0, 0), (0, 1), (1, 0), (3, 0), (1, 1), (3, 1), (2, 0), (2, 1))


def pick(table, index):
    if isinstance(index, int):
        return table[index]
    value = jnp.int32(table[0])
    for place in range(1, len(table)):
        value = jnp.where(index == place, jnp.int32(table[place]), value)
    return value


def when(condition, action):
    if isinstance(condition, bool):
        if condition:
            action()
    else:
        pl.when(condition)(action)


def band_at(me, index, sign):
    dx = pick([s[0] for s in BAND_STEPS], index)
    dy = pick([s[1] for s in BAND_STEPS], index)
    return (me // 4 + 4 + sign * dx) % 4 * 4 + (me % 4 + 4 + sign * dy) % 4


def frame_at(me, index, sign):
    dz = pick([s[0] for s in FRAME_STEPS], index)
    dc = pick([s[1] for s in FRAME_STEPS], index)
    return (me // 2 + 4 + sign * dz) % 4 * 2 + (me % 2 + dc) % 2


def score_tile(query, keys, marks, scores, tops):
    running = None
    for start in range(0, TOKENS, CHUNK):
        first = start // TILE
        key = keys[pl.ds(first, CHUNK // TILE), 0].reshape(CHUNK, HD)
        key = jnp.concatenate([key, marks[pl.ds(start, CHUNK), :]], axis=1)
        part = lax.dot_general(query, key, NT, preferred_element_type=F32)
        scores[:, pl.ds(start, CHUNK)] = part
        for lane in range(0, CHUNK, 128):
            piece = part[:, lane : lane + 128]
            running = piece if running is None else jnp.maximum(running, piece)
    top = jnp.max(running, axis=1, keepdims=True)
    tops[...] = jnp.broadcast_to(top, tops.shape)


def value_tile(scores, tops, values):
    top = jnp.concatenate([tops[...]] * (CHUNK // 128), axis=1)
    total = None
    ones = jnp.ones((CHUNK, HD), BF16)
    for start in range(0, TOKENS, CHUNK):
        first = start // TILE
        value = values[pl.ds(first, CHUNK // TILE), 1].reshape(CHUNK, HD)
        value = jnp.concatenate([value, ones], axis=1)
        weights = jnp.exp2((scores[:, pl.ds(start, CHUNK)] - top) * EXPONENT).astype(BF16)
        part = jnp.dot(weights, value, preferred_element_type=F32)
        total = part if total is None else total + part
    return (total[:, :HD] / total[:, HD:]).astype(BF16)


def kernel(
    q_hbm, k_hbm, v_hbm, ints_hbm,
    out,
    q_in, k_in, v_in, q_send, kv_send, qt_send, kvt_send, row_send,
    q_got, kv_got, row_got, o_send, o_got0, o_got1, marks,
    scores0, scores1, tops0, tops1, ints, place, order,
    load_sem, send_sem, kv_sem, row_sem, q_sem, o_sem, osend_sem, groups_in, all_in,
):
    o_got = (o_got0, o_got1)
    group = lax.axis_index("frame")
    band = lax.axis_index("band")

    barrier = pltpu.get_barrier_semaphore()
    for i in range(15, 0, -1):
        pl.semaphore_signal(barrier, inc=1, device_id={"band": band_at(band, i, 1)}, device_id_type=MESH)

    leader = band % 4 == 0

    def greet_groups(sem):
        for i in range(1, 8):
            pl.semaphore_signal(sem, inc=1, device_id={"frame": frame_at(group, i, 1)}, device_id_type=MESH)

    pl.when(leader)(lambda: greet_groups(barrier))

    small = pltpu.make_async_copy(ints_hbm, ints, load_sem.at[3])
    small.start()
    def load(i, source, target):
        for h in range(HEADS):
            pltpu.make_async_copy(source.at[:, :, pl.ds(h * HD, HD)], target.at[h], load_sem.at[i]).start()
        return pltpu.make_async_copy(target, target, load_sem.at[i])

    k_load = load(0, k_hbm, k_in)
    v_load = load(1, v_hbm, v_in)
    small.wait()
    before = jnp.int32(0)
    counts = []
    for h in range(HEADS):
        here = ints[1, 2, h]
        place[h] = jnp.minimum(here * before + (1 - here) * (SPATIAL + h - before), HEADS - 1)
        before = before + here
        counts.append(before)

    def fill(slot, carry):
        spatial, temporal = jnp.int32(0), jnp.int32(0)
        for h in range(HEADS):
            spatial = spatial + (counts[h] <= slot).astype(jnp.int32)
            temporal = temporal + (h + 1 - counts[h] <= slot).astype(jnp.int32)
        order[slot] = jnp.minimum(spatial, HEADS - 1)

        @pl.when(slot < TEMPORAL)
        def _():
            order[SPATIAL + slot] = jnp.minimum(temporal, HEADS - 1)

        return carry

    lax.fori_loop(0, SPATIAL, fill, 0)

    lane = lax.broadcasted_iota(jnp.int32, (1, 128), 1)
    for kind in range(2):
        for f in range(2):
            row = jnp.zeros((1, 128), F32)
            for t in range(TILES):
                row = jnp.where(lane == t, (1 - ints[f, kind, t]).astype(F32) * NEGATIVE, row)
            row_send[kind, f] = row
            if kind == 0:
                row_got[f, band] = row
            else:
                row_got[2, 2 * group + f] = row

    def head(ref, f, slot):
        return ref[order[slot], f]

    def send(source, target, device, sent, got):
        pltpu.make_async_remote_copy(
            src_ref=source,
            dst_ref=target,
            send_sem=sent,
            recv_sem=got,
            device_id=device,
            device_id_type=MESH,
        ).start()

    def send_rows(kind):
        for i in range(1, 16 - 8 * kind):
            if kind == 0:
                target, device = row_got.at[pl.ds(0, 2), band], {"band": band_at(band, i, 1)}
            else:
                target, device = row_got.at[2, pl.ds(2 * group, 2)], {"frame": frame_at(group, i, 1)}
            send(row_send.at[kind], target, device, send_sem.at[2, kind], row_sem.at[kind])

    def keep_own(f):
        kv_got[f, band, 0] = head(k_in, f, band)
        kv_got[f, band, 1] = head(v_in, f, band)
        q_got[f, band] = head(q_in, f, band)
        kv_got[2, 2 * group + f, 0] = head(k_in, f, SPATIAL + group)
        kv_got[2, 2 * group + f, 1] = head(v_in, f, SPATIAL + group)
        q_got[2, 2 * group + f] = head(q_in, f, SPATIAL + group)

    def send_keys(f, places):
        for i in places:
            dest = band_at(band, i, 1)
            kv_send[f, i, 0] = head(k_in, f, dest)
            kv_send[f, i, 1] = head(v_in, f, dest)
            send(kv_send.at[f, i], kv_got.at[f, band], {"band": dest}, send_sem.at[0, f], kv_sem.at[f])

    def send_queries(f, places):
        for i in places:
            dest = band_at(band, i, 1)
            q_send[f, i] = head(q_in, f, dest)
            send(q_send.at[f, i], q_got.at[f, band], {"band": dest}, send_sem.at[1, f], q_sem.at[f, i])

    def send_temporal():
        for i in range(1, 8):
            dest = frame_at(group, i, 1)
            for f in range(2):
                kvt_send[i, f, 0] = head(k_in, f, SPATIAL + dest)
                kvt_send[i, f, 1] = head(v_in, f, SPATIAL + dest)
            send(kvt_send.at[i], kv_got.at[2, pl.ds(2 * group, 2)], {"frame": dest}, send_sem.at[0, 2], kv_sem.at[2])
        for i in range(1, 8):
            dest = frame_at(group, i, 1)
            for f in range(2):
                qt_send[i, f] = head(q_in, f, SPATIAL + dest)
            send(qt_send.at[i], q_got.at[2, pl.ds(2 * group, 2)], {"frame": dest}, send_sem.at[1, 2], q_sem.at[2, i])

    everyone = range(1, 16)
    q_load = load(2, q_hbm, q_in)
    k_load.wait()
    v_load.wait()
    pl.when(band % 4 > 0)(lambda: pl.semaphore_wait(barrier, 15))

    @pl.when(leader)
    def _():
        pl.semaphore_wait(barrier, 22)
        greet_groups(groups_in)

    send_keys(0, everyone)
    send_rows(0)
    q_load.wait()
    send_queries(0, everyone)

    @pl.when(leader)
    def _():
        pl.semaphore_wait(groups_in, 7)
        for i in range(1, 4):
            pl.semaphore_signal(all_in, inc=1, device_id={"band": band + i}, device_id_type=MESH)

    pl.when(band % 4 > 0)(lambda: pl.semaphore_wait(all_in, 1))
    send_temporal()
    send_rows(1)
    send_keys(1, everyone)
    send_queries(1, everyone)
    keep_own(0)
    keep_own(1)

    lane = lax.broadcasted_iota(jnp.int32, (TILE, 128), 1)
    for t in range(TILES):
        marks[pl.ds(t * TILE, TILE), :] = jnp.where(lane == t, 1.0, 0.0).astype(BF16)

    def wait_bytes(ref, sem):
        pltpu.make_async_copy(ref, ref, sem).wait()

    def wait_keys(u):
        many = 15 if u < 2 else 14
        wait_bytes(kv_got.at[u, pl.ds(0, many)], kv_sem.at[u])

    def tiles_of(u, step):
        if u < 2:
            return band_at(band, 2 * step, -1), band_at(band, 2 * step + 1, -1)
        source = frame_at(group, step, -1)
        return 2 * source, 2 * source + 1

    def wait_query(u, step):
        if u < 2:

            def first():
                wait_bytes(q_got.at[u, 0], q_sem.at[u, 2 * step])

            when(step > 0, first)

            wait_bytes(q_got.at[u, 0], q_sem.at[u, 2 * step + 1])
        else:

            when(step > 0, lambda: wait_bytes(q_got.at[u, pl.ds(0, 2)], q_sem.at[u, step]))

    def run_scores(u, step, scores, tops):
        rows = []
        for t in tiles_of(u, step):
            bias = jnp.broadcast_to(row_got[u, t], (TILE, 128)).astype(BF16)
            rows.append(jnp.concatenate([q_got[u, t], bias], axis=1))
        score_tile(jnp.concatenate(rows, axis=0), kv_got.at[u], marks, scores, tops)

    def run_values(u, step, scores, tops):
        result = value_tile(scores, tops, kv_got.at[u])
        first, second = tiles_of(u, step)
        o_send[u, first] = result[:TILE]
        o_send[u, second] = result[TILE:]
        if u == 0:
            return
        if u < 2:
            for t, guarded in ((first, True), (second, False)):
                copy = pltpu.make_async_remote_copy(
                    src_ref=o_send.at[u, t],
                    dst_ref=o_got[u].at[band],
                    send_sem=osend_sem.at[u],
                    recv_sem=o_sem.at[u],
                    device_id={"band": t},
                    device_id_type=MESH,
                )
                if guarded:
                    when(step > 0, copy.start)
                else:
                    copy.start()
        else:
            for f in range(2):
                copy = pltpu.make_async_remote_copy(
                    src_ref=o_send.at[2, first + f],
                    dst_ref=o_got[f].at[SPATIAL + group],
                    send_sem=osend_sem.at[u],
                    recv_sem=o_sem.at[u],
                    device_id={"frame": first // 2},
                    device_id_type=MESH,
                )
                when(step > 0, copy.start)

    def run_unit(u):
        wait_keys(u)
        if u == 1:
            for i in range(1, 16):
                t = band_at(band, i, -1)
                pltpu.make_async_remote_copy(
                    src_ref=o_send.at[0, t],
                    dst_ref=o_got0.at[band],
                    send_sem=osend_sem.at[0],
                    recv_sem=o_sem.at[0],
                    device_id={"band": t},
                    device_id_type=MESH,
                ).start()
        wait_query(u, 0)
        run_scores(u, 0, scores0, tops0)

        def body(i, carry):
            wait_query(u, 2 * i + 1)
            run_scores(u, 2 * i + 1, scores1, tops1)
            run_values(u, 2 * i, scores0, tops0)

            wait_query(u, 2 * i + 2)
            run_scores(u, 2 * i + 2, scores0, tops0)
            run_values(u, 2 * i + 1, scores1, tops1)
            return carry

        lax.fori_loop(0, 3, body, 0)
        wait_query(u, 7)
        run_scores(u, 7, scores1, tops1)
        run_values(u, 6, scores0, tops0)
        run_values(u, 7, scores1, tops1)

    wait_bytes(row_got.at[pl.ds(0, 2), pl.ds(0, 15)], row_sem.at[0])
    run_unit(0)
    wait_bytes(row_got.at[2, pl.ds(0, 14)], row_sem.at[1])
    run_unit(2)
    run_unit(1)

    for f in range(2):
        o_got[f][band] = o_send[f, band]
        o_got[f][SPATIAL + group] = o_send[2, 2 * group + f]

    wait_bytes(o_send.at[2, pl.ds(0, 14)], o_sem.at[2])
    for f in range(2):
        wait_bytes(o_send.at[f, pl.ds(0, 15)], o_sem.at[f])
        for h in range(HEADS):
            out[f, :, pl.ds(h * HD, HD)] = o_got[f][place[h]]

    for f in range(2):
        wait_bytes(kv_send.at[f, pl.ds(1, 15)], send_sem.at[0, f])
        wait_bytes(q_send.at[f, pl.ds(1, 15)], send_sem.at[1, f])
    wait_bytes(kvt_send.at[pl.ds(1, 7)], send_sem.at[0, 2])
    wait_bytes(qt_send.at[pl.ds(1, 7)], send_sem.at[1, 2])
    wait_bytes(row_got.at[pl.ds(0, 2), pl.ds(0, 15)], send_sem.at[2, 0])
    wait_bytes(row_got.at[2, pl.ds(0, 14)], send_sem.at[2, 1])
    for u, many in ((0, 15), (1, 15), (2, 14)):
        wait_bytes(o_send.at[u, pl.ds(0, many)], osend_sem.at[u])


def body(queries, keys, values, head_kind, spatial_mask, temporal_mask):
    vmem, sem = pltpu.VMEM, pltpu.SemaphoreType.DMA
    hbm = pl.BlockSpec(memory_space=pltpu.HBM)
    wide = HEADS - TILES
    ints = (
        jnp.pad(spatial_mask, ((0, 0), (0, 2), (0, wide)))
        + jnp.pad(temporal_mask.transpose(1, 0, 2), ((0, 0), (1, 1), (0, wide)))
        + jnp.pad(head_kind.reshape(1, 1, HEADS), ((1, 0), (2, 0), (0, 0)))
    )
    return pl.pallas_call(
        kernel,
        out_shape=jax.ShapeDtypeStruct(queries.shape, BF16),
        in_specs=[hbm] * 4,
        out_specs=pl.BlockSpec(memory_space=pltpu.VMEM),
        scratch_shapes=[
            vmem((HEADS, 2, TILE, HD), BF16), vmem((HEADS, 2, TILE, HD), BF16), vmem((HEADS, 2, TILE, HD), BF16),
            vmem((2, 16, TILE, HD), BF16), vmem((2, 16, 2, TILE, HD), BF16),
            vmem((8, 2, TILE, HD), BF16), vmem((8, 2, 2, TILE, HD), BF16), vmem((2, 2, 1, 128), F32),
            vmem((3, TILES, TILE, HD), BF16), vmem((3, TILES, 2, TILE, HD), BF16), vmem((3, TILES, 1, 128), F32),
            vmem((3, TILES, TILE, HD), BF16), vmem((HEADS, TILE, HD), BF16), vmem((HEADS, TILE, HD), BF16),
            vmem((TOKENS, 128), BF16),
            vmem((256, TOKENS), F32), vmem((256, TOKENS), F32), vmem((256, 128), F32), vmem((256, 128), F32),
            pltpu.SMEM((2, 3, HEADS), jnp.int32),
            pltpu.SMEM((HEADS,), jnp.int32), pltpu.SMEM((HEADS,), jnp.int32),
            sem((4,)), sem((3, 3)), sem((3,)), sem((2,)), sem((3, 16)), sem((3,)), sem((3,)),
            pltpu.SemaphoreType.REGULAR, pltpu.SemaphoreType.REGULAR,
        ],
        compiler_params=pltpu.CompilerParams(
            collective_id=0, has_side_effects=True, vmem_limit_bytes=52 * 2**20
        ),
        cost_estimate=pl.CostEstimate(flops=6442450944, bytes_accessed=6291456, transcendentals=12582912),
    )(queries, keys, values, ints)


def solution(mesh):
    return jax.shard_map(
        body,
        mesh=mesh,
        in_specs=(
            P("frame", "band", None),
            P("frame", "band", None),
            P("frame", "band", None),
            P(),
            P("frame", "band", None),
            P("band", "frame", None),
        ),
        out_specs=P("frame", "band", None),
        check_vma=False,
    )
```

```python
import functools
import math

import jax
import jax.numpy as jnp
from jax import lax
from jax.experimental import pallas as pl
from jax.experimental.pallas import tpu as pltpu
from jax.sharding import PartitionSpec as P

MESH = pl.DeviceIdType.MESH
HD = 128
HEADS = 24
SPATIAL = 16
TEMPORAL = HEADS - SPATIAL
TILE = 128
TILES = 16
TOKENS = TILES * TILE
NEGATIVE = -1e30
EXPONENT = math.log2(math.e) / math.sqrt(HD)
CHUNK = 512
NT = (((1,), (1,)), ((), ()))
BF16 = jnp.bfloat16
F32 = jnp.float32

BAND_STEPS = (
    (0, 0), (1, 0), (2, 1), (3, 3), (0, 3), (1, 2), (3, 1), (2, 0),
    (3, 0), (2, 3), (1, 1), (0, 1), (3, 2), (1, 3), (0, 2), (2, 2),
)
FRAME_STEPS = ((0, 0), (0, 1), (1, 0), (3, 0), (1, 1), (3, 1), (2, 0), (2, 1))


def pick(table, index):
    if isinstance(index, int):
        return table[index]
    value = jnp.int32(table[0])
    for place in range(1, len(table)):
        value = jnp.where(index == place, jnp.int32(table[place]), value)
    return value


def when(condition, action):
    if isinstance(condition, bool):
        if condition:
            action()
    else:
        pl.when(condition)(action)


def band_at(me, index, sign):
    dx = pick([s[0] for s in BAND_STEPS], index)
    dy = pick([s[1] for s in BAND_STEPS], index)
    return (me // 4 + 4 + sign * dx) % 4 * 4 + (me % 4 + 4 + sign * dy) % 4


def frame_at(me, index, sign):
    dz = pick([s[0] for s in FRAME_STEPS], index)
    dc = pick([s[1] for s in FRAME_STEPS], index)
    return (me // 2 + 4 + sign * dz) % 4 * 2 + (me % 2 + dc) % 2


def score_tile(query, keys, marks, scores, tops):
    running = None
    for start in range(0, TOKENS, CHUNK):
        first = start // TILE
        key = keys[pl.ds(first, CHUNK // TILE), 0].reshape(CHUNK, HD)
        key = jnp.concatenate([key, marks[pl.ds(start, CHUNK), :]], axis=1)
        part = lax.dot_general(query, key, NT, preferred_element_type=F32)
        scores[:, pl.ds(start, CHUNK)] = part
        for lane in range(0, CHUNK, 128):
            piece = part[:, lane : lane + 128]
            running = piece if running is None else jnp.maximum(running, piece)
    top = jnp.max(running, axis=1, keepdims=True)
    tops[...] = jnp.broadcast_to(top, tops.shape)


def value_tile(scores, tops, values):
    top = jnp.concatenate([tops[...]] * (CHUNK // 128), axis=1)
    total = None
    ones = jnp.ones((CHUNK, HD), BF16)
    for start in range(0, TOKENS, CHUNK):
        first = start // TILE
        value = values[pl.ds(first, CHUNK // TILE), 1].reshape(CHUNK, HD)
        value = jnp.concatenate([value, ones], axis=1)
        weights = jnp.exp2((scores[:, pl.ds(start, CHUNK)] - top) * EXPONENT).astype(BF16)
        part = jnp.dot(weights, value, preferred_element_type=F32)
        total = part if total is None else total + part
    return (total[:, :HD] / total[:, HD:]).astype(BF16)


def kernel(
    q_hbm, k_hbm, v_hbm, ints_hbm,
    out,
    q_in, k_in, v_in, q_send, kv_send, qt_send, kvt_send, row_send,
    q_got, kv_got, row_got, o_send, o_got0, o_got1, marks,
    scores0, scores1, tops0, tops1, ints, place, order,
    load_sem, send_sem, kv_sem, row_sem, q_sem, o_sem, osend_sem, groups_in, all_in,
):
    o_got = (o_got0, o_got1)
    group = lax.axis_index("frame")
    band = lax.axis_index("band")

    barrier = pltpu.get_barrier_semaphore()
    for i in range(15, 0, -1):
        pl.semaphore_signal(barrier, inc=1, device_id={"band": band_at(band, i, 1)}, device_id_type=MESH)

    leader = band % 4 == 0

    def greet_groups(sem):
        for i in range(1, 8):
            pl.semaphore_signal(sem, inc=1, device_id={"frame": frame_at(group, i, 1)}, device_id_type=MESH)

    pl.when(leader)(lambda: greet_groups(barrier))

    small = pltpu.make_async_copy(ints_hbm, ints, load_sem.at[3])
    small.start()
    def load(i, source, target):
        for h in range(HEADS):
            pltpu.make_async_copy(source.at[:, :, pl.ds(h * HD, HD)], target.at[h], load_sem.at[i]).start()
        return pltpu.make_async_copy(target, target, load_sem.at[i])

    k_load = load(0, k_hbm, k_in)
    v_load = load(1, v_hbm, v_in)
    small.wait()
    before = jnp.int32(0)
    counts = []
    for h in range(HEADS):
        here = ints[1, 2, h]
        place[h] = jnp.minimum(here * before + (1 - here) * (SPATIAL + h - before), HEADS - 1)
        before = before + here
        counts.append(before)

    def fill(slot, carry):
        spatial, temporal = jnp.int32(0), jnp.int32(0)
        for h in range(HEADS):
            spatial = spatial + (counts[h] <= slot).astype(jnp.int32)
            temporal = temporal + (h + 1 - counts[h] <= slot).astype(jnp.int32)
        order[slot] = jnp.minimum(spatial, HEADS - 1)

        @pl.when(slot < TEMPORAL)
        def _():
            order[SPATIAL + slot] = jnp.minimum(temporal, HEADS - 1)

        return carry

    lax.fori_loop(0, SPATIAL, fill, 0)

    lane = lax.broadcasted_iota(jnp.int32, (1, 128), 1)
    for kind in range(2):
        for f in range(2):
            row = jnp.zeros((1, 128), F32)
            for t in range(TILES):
                row = jnp.where(lane == t, (1 - ints[f, kind, t]).astype(F32) * NEGATIVE, row)
            row_send[kind, f] = row
            if kind == 0:
                row_got[f, band] = row
            else:
                row_got[2, 2 * group + f] = row

    def head(ref, f, slot):
        return ref[order[slot], f]

    def send(source, target, device, sent, got):
        pltpu.make_async_remote_copy(
            src_ref=source,
            dst_ref=target,
            send_sem=sent,
            recv_sem=got,
            device_id=device,
            device_id_type=MESH,
        ).start()

    def send_rows(kind):
        for i in range(1, 16 - 8 * kind):
            if kind == 0:
                target, device = row_got.at[pl.ds(0, 2), band], {"band": band_at(band, i, 1)}
            else:
                target, device = row_got.at[2, pl.ds(2 * group, 2)], {"frame": frame_at(group, i, 1)}
            send(row_send.at[kind], target, device, send_sem.at[2, kind], row_sem.at[kind])

    def keep_own(f):
        kv_got[f, band, 0] = head(k_in, f, band)
        kv_got[f, band, 1] = head(v_in, f, band)
        q_got[f, band] = head(q_in, f, band)
        kv_got[2, 2 * group + f, 0] = head(k_in, f, SPATIAL + group)
        kv_got[2, 2 * group + f, 1] = head(v_in, f, SPATIAL + group)
        q_got[2, 2 * group + f] = head(q_in, f, SPATIAL + group)

    def send_keys(f, places):
        for i in places:
            dest = band_at(band, i, 1)
            kv_send[f, i, 0] = head(k_in, f, dest)
            kv_send[f, i, 1] = head(v_in, f, dest)
            send(kv_send.at[f, i], kv_got.at[f, band], {"band": dest}, send_sem.at[0, f], kv_sem.at[f])

    def send_queries(f, places):
        for i in places:
            dest = band_at(band, i, 1)
            q_send[f, i] = head(q_in, f, dest)
            send(q_send.at[f, i], q_got.at[f, band], {"band": dest}, send_sem.at[1, f], q_sem.at[f, i])

    def send_temporal():
        for i in range(1, 8):
            dest = frame_at(group, i, 1)
            for f in range(2):
                kvt_send[i, f, 0] = head(k_in, f, SPATIAL + dest)
                kvt_send[i, f, 1] = head(v_in, f, SPATIAL + dest)
            send(kvt_send.at[i], kv_got.at[2, pl.ds(2 * group, 2)], {"frame": dest}, send_sem.at[0, 2], kv_sem.at[2])
        for i in range(1, 8):
            dest = frame_at(group, i, 1)
            for f in range(2):
                qt_send[i, f] = head(q_in, f, SPATIAL + dest)
            send(qt_send.at[i], q_got.at[2, pl.ds(2 * group, 2)], {"frame": dest}, send_sem.at[1, 2], q_sem.at[2, i])

    everyone = range(1, 16)
    q_load = load(2, q_hbm, q_in)
    k_load.wait()
    v_load.wait()
    pl.when(band % 4 > 0)(lambda: pl.semaphore_wait(barrier, 15))

    @pl.when(leader)
    def _():
        pl.semaphore_wait(barrier, 22)
        greet_groups(groups_in)

    send_keys(0, everyone)
    send_rows(0)
    q_load.wait()
    send_queries(0, everyone)

    @pl.when(leader)
    def _():
        pl.semaphore_wait(groups_in, 7)
        for i in range(1, 4):
            pl.semaphore_signal(all_in, inc=1, device_id={"band": band + i}, device_id_type=MESH)

    pl.when(band % 4 > 0)(lambda: pl.semaphore_wait(all_in, 1))
    send_temporal()
    send_rows(1)
    send_keys(1, everyone)
    send_queries(1, everyone)
    keep_own(0)
    keep_own(1)

    lane = lax.broadcasted_iota(jnp.int32, (TILE, 128), 1)
    for t in range(TILES):
        marks[pl.ds(t * TILE, TILE), :] = jnp.where(lane == t, 1.0, 0.0).astype(BF16)

    def wait_bytes(ref, sem):
        pltpu.make_async_copy(ref, ref, sem).wait()

    def wait_keys(u):
        many = 15 if u < 2 else 14
        wait_bytes(kv_got.at[u, pl.ds(0, many)], kv_sem.at[u])

    def tiles_of(u, step):
        if u < 2:
            return band_at(band, 2 * step, -1), band_at(band, 2 * step + 1, -1)
        source = frame_at(group, step, -1)
        return 2 * source, 2 * source + 1

    def wait_query(u, step):
        if u < 2:

            def first():
                wait_bytes(q_got.at[u, 0], q_sem.at[u, 2 * step])

            when(step > 0, first)

            wait_bytes(q_got.at[u, 0], q_sem.at[u, 2 * step + 1])
        else:

            when(step > 0, lambda: wait_bytes(q_got.at[u, pl.ds(0, 2)], q_sem.at[u, step]))

    def run_scores(u, step, scores, tops):
        rows = []
        for t in tiles_of(u, step):
            bias = jnp.broadcast_to(row_got[u, t], (TILE, 128)).astype(BF16)
            rows.append(jnp.concatenate([q_got[u, t], bias], axis=1))
        score_tile(jnp.concatenate(rows, axis=0), kv_got.at[u], marks, scores, tops)

    def run_values(u, step, scores, tops):
        result = value_tile(scores, tops, kv_got.at[u])
        first, second = tiles_of(u, step)
        o_send[u, first] = result[:TILE]
        o_send[u, second] = result[TILE:]
        if u == 0:
            return
        if u < 2:
            for t, guarded in ((first, True), (second, False)):
                copy = pltpu.make_async_remote_copy(
                    src_ref=o_send.at[u, t],
                    dst_ref=o_got[u].at[band],
                    send_sem=osend_sem.at[u],
                    recv_sem=o_sem.at[u],
                    device_id={"band": t},
                    device_id_type=MESH,
                )
                if guarded:
                    when(step > 0, copy.start)
                else:
                    copy.start()
        else:
            for f in range(2):
                copy = pltpu.make_async_remote_copy(
                    src_ref=o_send.at[2, first + f],
                    dst_ref=o_got[f].at[SPATIAL + group],
                    send_sem=osend_sem.at[u],
                    recv_sem=o_sem.at[u],
                    device_id={"frame": first // 2},
                    device_id_type=MESH,
                )
                when(step > 0, copy.start)

    def run_unit(u):
        if u == 1:
            for i in range(1, 16):
                t = band_at(band, i, -1)
                pltpu.make_async_remote_copy(
                    src_ref=o_send.at[0, t],
                    dst_ref=o_got0.at[band],
                    send_sem=osend_sem.at[0],
                    recv_sem=o_sem.at[0],
                    device_id={"band": t},
                    device_id_type=MESH,
                ).start()
        wait_keys(u)
        wait_query(u, 0)
        run_scores(u, 0, scores0, tops0)

        def body(i, carry):
            wait_query(u, 2 * i + 1)
            run_scores(u, 2 * i + 1, scores1, tops1)
            run_values(u, 2 * i, scores0, tops0)

            wait_query(u, 2 * i + 2)
            run_scores(u, 2 * i + 2, scores0, tops0)
            run_values(u, 2 * i + 1, scores1, tops1)
            return carry

        lax.fori_loop(0, 3, body, 0)
        wait_query(u, 7)
        run_scores(u, 7, scores1, tops1)
        run_values(u, 6, scores0, tops0)
        run_values(u, 7, scores1, tops1)

    wait_bytes(row_got.at[pl.ds(0, 2), pl.ds(0, 15)], row_sem.at[0])
    run_unit(0)
    wait_bytes(row_got.at[2, pl.ds(0, 14)], row_sem.at[1])
    run_unit(2)
    run_unit(1)

    for f in range(2):
        o_got[f][band] = o_send[f, band]
        o_got[f][SPATIAL + group] = o_send[2, 2 * group + f]

    wait_bytes(o_send.at[2, pl.ds(0, 14)], o_sem.at[2])
    for f in range(2):
        wait_bytes(o_send.at[f, pl.ds(0, 15)], o_sem.at[f])
        for h in range(HEADS):
            out[f, :, pl.ds(h * HD, HD)] = o_got[f][place[h]]

    for f in range(2):
        wait_bytes(kv_send.at[f, pl.ds(1, 15)], send_sem.at[0, f])
        wait_bytes(q_send.at[f, pl.ds(1, 15)], send_sem.at[1, f])
    wait_bytes(kvt_send.at[pl.ds(1, 7)], send_sem.at[0, 2])
    wait_bytes(qt_send.at[pl.ds(1, 7)], send_sem.at[1, 2])
    wait_bytes(row_got.at[pl.ds(0, 2), pl.ds(0, 15)], send_sem.at[2, 0])
    wait_bytes(row_got.at[2, pl.ds(0, 14)], send_sem.at[2, 1])
    for u, many in ((0, 15), (1, 15), (2, 14)):
        wait_bytes(o_send.at[u, pl.ds(0, many)], osend_sem.at[u])


def body(queries, keys, values, head_kind, spatial_mask, temporal_mask):
    vmem, sem = pltpu.VMEM, pltpu.SemaphoreType.DMA
    hbm = pl.BlockSpec(memory_space=pltpu.HBM)
    wide = HEADS - TILES
    ints = (
        jnp.pad(spatial_mask, ((0, 0), (0, 2), (0, wide)))
        + jnp.pad(temporal_mask.transpose(1, 0, 2), ((0, 0), (1, 1), (0, wide)))
        + jnp.pad(head_kind.reshape(1, 1, HEADS), ((1, 0), (2, 0), (0, 0)))
    )
    return pl.pallas_call(
        kernel,
        out_shape=jax.ShapeDtypeStruct(queries.shape, BF16),
        in_specs=[hbm] * 4,
        out_specs=pl.BlockSpec(memory_space=pltpu.VMEM),
        scratch_shapes=[
            vmem((HEADS, 2, TILE, HD), BF16), vmem((HEADS, 2, TILE, HD), BF16), vmem((HEADS, 2, TILE, HD), BF16),
            vmem((2, 16, TILE, HD), BF16), vmem((2, 16, 2, TILE, HD), BF16),
            vmem((8, 2, TILE, HD), BF16), vmem((8, 2, 2, TILE, HD), BF16), vmem((2, 2, 1, 128), F32),
            vmem((3, TILES, TILE, HD), BF16), vmem((3, TILES, 2, TILE, HD), BF16), vmem((3, TILES, 1, 128), F32),
            vmem((3, TILES, TILE, HD), BF16), vmem((HEADS, TILE, HD), BF16), vmem((HEADS, TILE, HD), BF16),
            vmem((TOKENS, 128), BF16),
            vmem((256, TOKENS), F32), vmem((256, TOKENS), F32), vmem((256, 128), F32), vmem((256, 128), F32),
            pltpu.SMEM((2, 3, HEADS), jnp.int32),
            pltpu.SMEM((HEADS,), jnp.int32), pltpu.SMEM((HEADS,), jnp.int32),
            sem((4,)), sem((3, 3)), sem((3,)), sem((2,)), sem((3, 16)), sem((3,)), sem((3,)),
            pltpu.SemaphoreType.REGULAR, pltpu.SemaphoreType.REGULAR,
        ],
        compiler_params=pltpu.CompilerParams(
            collective_id=0, has_side_effects=True, vmem_limit_bytes=52 * 2**20
        ),
        cost_estimate=pl.CostEstimate(flops=6442450944, bytes_accessed=6291456, transcendentals=12582912),
    )(queries, keys, values, ints)


def solution(mesh):
    return jax.shard_map(
        body,
        mesh=mesh,
        in_specs=(
            P("frame", "band", None),
            P("frame", "band", None),
            P("frame", "band", None),
            P(),
            P("frame", "band", None),
            P("band", "frame", None),
        ),
        out_specs=P("frame", "band", None),
        check_vma=False,
    )
```
